32 devices in a mesh: sample: 4 (over y, x), feat: 8 (over z, core).
Axes of the slice: x: 2, y: 2, z: 4, core: 2. Of those that a mesh axis runs over, the one named last changes fastest.
Arguments:
- view_a: bfloat16 [512, 16384], P('sample', 'feat'), may hold values from -60 to 60
- view_b: bfloat16 [512, 16384], P('sample', 'feat'), may hold values from -60 to 60
Outputs:
- loss: float32 [], replicated
- grad_a: bfloat16 [512, 16384], P('sample', 'feat')
- grad_b: bfloat16 [512, 16384], P('sample', 'feat')
The draws below stay inside these ranges and needn't reach their ends.
All inputs are finite; a program needn't handle non-finite values.
Results may differ from the reference program's by a relative error of at most 0.02.
Values may be sent and summed in bfloat16 or wider, within the bound.
A program may use at most 128 MiB of HBM per device.

```python
import math
import jax
import jax.numpy as jnp
from jax import lax

F = 16384
BATCH = 512
N_SAMPLE = 4
N_FEAT = 8


def pair_views(key):
    subkeys = jax.random.split(jax.random.fold_in(key, 11), 9)
    block_width = F // N_FEAT
    feature_pos = (jnp.arange(F, dtype=jnp.int32) % block_width).astype(jnp.float32) / block_width
    private_a = jax.random.normal(subkeys[0], (BATCH, F), jnp.float32)
    private_b = jax.random.normal(subkeys[1], (BATCH, F), jnp.float32)
    shared_weight = 0.35
    row_top = math.log(3.0)
    mix_top = 0.95
    mix_fall = 0.75
    load_rise = math.log(3.0)
    common_rows = jax.random.normal(subkeys[2], (BATCH, 1), jnp.float32)
    loading = jax.random.normal(subkeys[3], (1, F), jnp.float32) * jnp.exp(load_rise * feature_pos)[None, :]
    row_pos = jnp.arange(BATCH, dtype=jnp.float32) / max(BATCH - 1, 1)
    row_scale = jnp.exp(row_top * row_pos)[:, None] * jax.random.uniform(subkeys[4], (BATCH, 1), jnp.float32, 0.7, 1.4)
    mixing = (mix_top - mix_fall * feature_pos)[None, :] * jax.random.uniform(subkeys[5], (1, F), jnp.float32, 0.75, 1.0)
    scale_a = jnp.exp(jax.random.uniform(subkeys[6], (1, F), jnp.float32, math.log(0.5), math.log(3.0)))
    scale_b = jnp.exp(jax.random.uniform(subkeys[7], (1, F), jnp.float32, math.log(0.5), math.log(3.0)))
    offsets = jax.random.normal(subkeys[8], (2, F), jnp.float32)
    shared = shared_weight * common_rows * loading
    signal_a = private_a + shared
    signal_b = mixing * private_a + jnp.sqrt(1.0 - mixing * mixing) * private_b + shared
    first = jnp.clip(offsets[0][None, :] + scale_a * row_scale * signal_a, -60.0, 60.0)
    second = jnp.clip(offsets[1][None, :] + scale_b * row_scale * signal_b, -60.0, 60.0)
    return (first, second)


def draw_view_a(key, part):
    return pair_views(key)[0].astype(jnp.bfloat16)


def draw_view_b(key, part):
    return pair_views(key)[1].astype(jnp.bfloat16)


def setup_inputs(seed: int = 0) -> dict:
    seeds = jax.random.split(jax.random.key(seed), 3)
    return {
        "view_a": draw_view_a(jax.random.fold_in(seeds[2], 71), 0),
        "view_b": draw_view_b(jax.random.fold_in(seeds[2], 71), 0),
    }


EPSILON = 1e-05
OFF_WEIGHT = 0.0051

def normalize(raw):
    floats = raw.astype(jnp.float32)
    mean_val = lax.optimization_barrier(jnp.mean(floats, axis=0))
    variance = lax.optimization_barrier(jnp.mean(floats * floats, axis=0)) - mean_val * mean_val
    scale_inv = lax.rsqrt(variance + EPSILON)
    return (((floats - mean_val) * scale_inv).astype(jnp.bfloat16), scale_inv)

def backnorm(grad_norm, normed, scale_inv):
    floats = normed.astype(jnp.float32)
    mean_grad = lax.optimization_barrier(jnp.mean(grad_norm, axis=0))
    mean_cross = lax.optimization_barrier(jnp.mean(grad_norm * floats, axis=0))
    return (scale_inv * (grad_norm - mean_grad - floats * mean_cross)).astype(jnp.bfloat16)

def reference(view_a, view_b):
    norm_a, scale_a = normalize(view_a)
    norm_b, scale_b = normalize(view_b)
    total_rows = view_a.shape[0]
    feature_count = view_a.shape[1]
    inv_rows = 1.0 / total_rows
    float_a = norm_a.astype(jnp.float32)
    float_b = norm_b.astype(jnp.float32)
    block_rows = feature_count // N_FEAT
    sub_width = block_rows // N_SAMPLE
    split_b = float_b.reshape(total_rows, N_FEAT, N_SAMPLE, sub_width)
    column_ids = jnp.arange(feature_count, dtype=jnp.int32)

    def block_step(folded, block_id):
        loss_sum, grad_nb = folded
        first_row = (block_id * block_rows).astype(jnp.int32)
        rows_a = lax.dynamic_slice_in_dim(float_a, first_row, block_rows, 1)
        correlation = jnp.dot(rows_a.T, float_b, precision=lax.Precision.HIGHEST) * inv_rows
        row_ids = first_row + jnp.arange(block_rows, dtype=jnp.int32)
        on_diagonal = row_ids[:, None] == column_ids[None, :]
        missing = 1.0 - correlation
        piece_loss = jnp.sum(jnp.where(on_diagonal, missing * missing, OFF_WEIGHT * correlation * correlation))
        factor = jnp.where(on_diagonal, correlation - 1.0, OFF_WEIGHT * correlation).astype(jnp.bfloat16)
        factor_wide = factor.astype(jnp.float32)
        split_factor = factor_wide.reshape(block_rows, N_FEAT, N_SAMPLE, sub_width)
        parts = jnp.einsum('nbsk,rbsk->snr', split_b, split_factor, precision=lax.Precision.HIGHEST)
        grad_block = lax.optimization_barrier(jnp.sum(parts.astype(jnp.bfloat16).astype(jnp.float32), axis=0))
        piece = jnp.dot(rows_a, factor_wide, precision=lax.Precision.HIGHEST)
        grad_nb = grad_nb + piece.astype(jnp.bfloat16).astype(jnp.float32)
        return ((loss_sum + piece_loss, grad_nb), grad_block)
    initial = (jnp.zeros((), jnp.float32), jnp.zeros((total_rows, feature_count), jnp.float32))
    (loss_sum, grad_nb), grad_blocks = lax.scan(block_step, initial, jnp.arange(N_FEAT, dtype=jnp.int32))
    grad_na = jnp.transpose(grad_blocks, (1, 0, 2)).reshape(total_rows, feature_count)
    loss = loss_sum / feature_count
    return (loss, backnorm(grad_na, norm_a, scale_a), backnorm(grad_nb, norm_b, scale_b))
```

```python
import jax
import jax.numpy as jnp
from jax import lax
from jax.sharding import PartitionSpec as P

EPSILON = 1e-05
OFF_WEIGHT = 0.0051


def gram(x):
    return lax.dot_general(x, x, (((1,), (1,)), ((), ())), preferred_element_type=jnp.float32)


def apply_gram(g, x):
    high = g.astype(jnp.bfloat16)
    low = (g - high.astype(jnp.float32)).astype(jnp.bfloat16)
    dims = (((1,), (0,)), ((), ()))
    return lax.dot_general(
        high, x, dims, preferred_element_type=jnp.float32
    ) + lax.dot_general(low, x, dims, preferred_element_type=jnp.float32)


def normalize(raw, inv_rows):
    floats = raw.astype(jnp.float32)
    mean = jnp.sum(floats, axis=0) * inv_rows
    scale = lax.rsqrt(jnp.sum(floats * floats, axis=0) * inv_rows - mean * mean + EPSILON)
    return ((floats - mean) * scale).astype(jnp.bfloat16), scale


def backnorm(grad, normed, scale, inv_rows):
    floats = normed.astype(jnp.float32)
    mean_grad = jnp.sum(grad, axis=0) * inv_rows
    mean_cross = jnp.sum(grad * floats, axis=0) * inv_rows
    return (scale * (grad - mean_grad - floats * mean_cross)).astype(jnp.bfloat16)


def body(view_a, view_b):
    rows_dev, cols_dev = view_a.shape
    groups = lax.axis_size("sample")
    blocks = lax.axis_size("feat")
    total_rows = rows_dev * groups
    features = cols_dev * blocks
    inv_rows = 1.0 / total_rows
    views = lax.all_to_all(
        jnp.stack((view_a, view_b)), "sample", split_axis=2, concat_axis=1, tiled=True
    )
    norm_a, scale_a = normalize(views[0], inv_rows)
    norm_b, scale_b = normalize(views[1], inv_rows)
    diag = jnp.sum(norm_a.astype(jnp.float32) * norm_b.astype(jnp.float32), axis=0) * inv_rows
    diag_loss = jnp.sum((1.0 - diag) * (1.0 - diag) - OFF_WEIGHT * diag * diag)
    grams, diag_loss = lax.psum(
        (jnp.stack((gram(norm_a), gram(norm_b))), diag_loss), ("sample", "feat")
    )
    all_loss = jnp.sum(grams[0] * grams[1]) * (OFF_WEIGHT * inv_rows * inv_rows)
    loss = (diag_loss + all_loss) / features
    extra = (1.0 - OFF_WEIGHT) * diag - 1.0
    weight = OFF_WEIGHT * inv_rows
    grad_na = weight * apply_gram(grams[1], norm_a) + extra * norm_b.astype(jnp.float32)
    grad_nb = weight * apply_gram(grams[0], norm_b) + extra * norm_a.astype(jnp.float32)
    grads = jnp.stack(
        (
            backnorm(grad_na, norm_a, scale_a, inv_rows),
            backnorm(grad_nb, norm_b, scale_b, inv_rows),
        )
    )
    grads = lax.all_to_all(grads, "sample", split_axis=1, concat_axis=2, tiled=True)
    return (loss, grads[0], grads[1])


def solution(mesh):
    in_specs = (P("sample", "feat"), P("sample", "feat"))
    out_specs = (P(), P("sample", "feat"), P("sample", "feat"))
    return jax.shard_map(body, mesh=mesh, in_specs=in_specs, out_specs=out_specs, check_vma=False)
```

```python
import functools

import jax
import jax.numpy as jnp
from jax import lax
from jax.experimental import pallas as pl
from jax.experimental.pallas import tpu as pltpu
from jax.sharding import PartitionSpec as P

EPSILON = 1e-05
OFF_WEIGHT = 0.0051
BLOCK = 128
CORES = 2
MESH = pl.DeviceIdType.MESH


def kernel(
    groups,
    blocks,
    view_a,
    view_b,
    out,
    loss_out,
    raw,
    norm,
    scales,
    extra,
    acc,
    send_core,
    recv_core,
    send_sample,
    recv_sample,
    send_depth,
    recv_depth,
    gram,
    full,
    grads,
    loss_core,
    loss_sample,
    loss_depth,
    send_sem,
    recv_sem,
    local_sem,
):
    rows_dev, cols_dev = view_a.shape
    total_rows = rows_dev * groups
    width = cols_dev // groups
    depth = blocks // CORES
    inv_rows = 1.0 / total_rows
    n_blocks = total_rows // BLOCK
    used = n_blocks * (n_blocks + 1) // 2 * BLOCK
    packed = acc.shape[0]
    rows_sample = packed // groups
    rows_depth = rows_sample // depth
    s = lax.axis_index("sample")
    f = lax.axis_index("feat")
    z = lax.div(f, CORES)
    c = lax.rem(f, CORES)
    other = 1 - c
    sample_peers = [(lax.rem(s + d, groups), f) for d in range(1, groups)]
    depth_peers = [(s, lax.rem(z + d, depth) * CORES + c) for d in range(1, depth)]
    sibling = (s, z * CORES + other)
    peers = sample_peers + depth_peers + [sibling]

    barrier = pltpu.get_barrier_semaphore()
    for peer in peers:
        pl.semaphore_signal(barrier, inc=1, device_id=peer, device_id_type=MESH)
    pl.semaphore_wait(barrier, len(peers))

    started = []

    def send(src, dst, peer):
        n = len(started)
        copy = pltpu.make_async_remote_copy(
            src_ref=src,
            dst_ref=dst,
            send_sem=send_sem.at[n],
            recv_sem=recv_sem.at[n],
            device_id=peer,
            device_id_type=MESH,
        )
        copy.start()
        started.append(copy)
        return copy

    def at(index, size):
        return pl.ds(pl.multiple_of(index * size, size), size)

    arriving = []
    for v, view in enumerate((view_a, view_b)):
        copies = [
            send(view.at[:, at(peer[0], width)], raw.at[v, at(s, rows_dev), :], peer)
            for peer in sample_peers
        ]
        own = pltpu.make_async_copy(
            view.at[:, at(s, width)], raw.at[v, at(s, rows_dev), :], local_sem.at[v]
        )
        own.start()
        arriving.append((copies, own))

    lanes = [slice(k, k + BLOCK) for k in range(0, width, BLOCK)]
    for v, (copies, own) in enumerate(arriving):
        own.wait()
        for copy in copies:
            copy.wait_recv()
        for cs in lanes:
            x = raw[v, :, cs].astype(jnp.float32)
            mean = jnp.sum(x, axis=0, keepdims=True) * inv_rows
            square = jnp.sum(x * x, axis=0, keepdims=True) * inv_rows
            scale = lax.rsqrt(square - mean * mean + EPSILON)
            scales[v, :, cs] = scale
            norm[v, :, cs] = ((x - mean) * scale).astype(jnp.bfloat16)

    def gram_rows(v, i):
        return lax.dot_general(
            norm[v, i * BLOCK : (i + 1) * BLOCK, :],
            norm[v, : (i + 1) * BLOCK, :],
            (((1,), (1,)), ((), ())),
            preferred_element_type=jnp.float32,
        )

    def spot(i, j):
        first = (i * (i + 1) // 2 + j) * BLOCK
        return slice(first, first + BLOCK)

    if packed > used:
        send_core[used:, :] = jnp.zeros((packed - used, BLOCK), jnp.bfloat16)
        acc[used:, :] = jnp.zeros((packed - used, BLOCK), jnp.float32)
    for i in range(n_blocks):
        strip = gram_rows(other, i)
        for j in range(i + 1):
            send_core[spot(i, j), :] = strip[:, j * BLOCK : (j + 1) * BLOCK].astype(jnp.bfloat16)
    to_core = send(send_core, recv_core, sibling)
    for i in range(n_blocks):
        strip = gram_rows(c, i)
        for j in range(i + 1):
            acc[spot(i, j), :] = strip[:, j * BLOCK : (j + 1) * BLOCK]
    part = jnp.zeros((1, BLOCK), jnp.float32)
    for cs in lanes:
        a = norm[0, :, cs].astype(jnp.float32)
        b = norm[1, :, cs].astype(jnp.float32)
        diag = jnp.sum(a * b, axis=0, keepdims=True) * inv_rows
        extra[:, cs] = (1.0 - OFF_WEIGHT) * diag - 1.0
        part = part + (1.0 - diag) * (1.0 - diag) - OFF_WEIGHT * diag * diag
    loss_core[c] = jnp.broadcast_to(part, (8, BLOCK))
    loss_copy = send(loss_core.at[c], loss_core.at[c], sibling)

    def fold(slots):
        total = slots[0]
        for k in range(1, slots.shape[0]):
            total = total + slots[k]
        return total

    to_core.wait_recv()
    acc[...] = acc[...] + recv_core[...].astype(jnp.float32)
    send_sample[...] = acc[...].astype(jnp.bfloat16)
    to_sample = [
        send(send_sample.at[at(peer[0], rows_sample), :], recv_sample.at[k], peer)
        for k, peer in enumerate(sample_peers)
    ]
    loss_copy.wait_recv()
    loss_sample[s] = fold(loss_core)
    loss_copies = [send(loss_sample.at[s], loss_sample.at[s], peer) for peer in sample_peers]

    mine = at(s, rows_sample)
    total = acc[mine, :]
    for k, copy in enumerate(to_sample):
        copy.wait_recv()
        total = total + recv_sample[k].astype(jnp.float32)
    acc[mine, :] = total
    send_depth[...] = total.astype(jnp.bfloat16)
    to_depth = [
        send(
            send_depth.at[at(lax.div(peer[1], CORES), rows_depth), :], recv_depth.at[k], peer
        )
        for k, peer in enumerate(depth_peers)
    ]
    for copy in loss_copies:
        copy.wait_recv()
    loss_depth[z] = fold(loss_sample)
    loss_copies = [send(loss_depth.at[z], loss_depth.at[z], peer) for peer in depth_peers]

    mine_depth = at(s * depth + z, rows_depth)
    total = acc[mine_depth, :]
    for k, copy in enumerate(to_depth):
        copy.wait_recv()
        total = total + recv_depth[k].astype(jnp.float32)
    gram[c, mine_depth, :] = total.astype(jnp.bfloat16)
    here = gram.at[c, mine_depth, :]
    for copy in [send(here, here, peer) for peer in depth_peers]:
        copy.wait_recv()
    here = gram.at[c, mine, :]
    for copy in [send(here, here, peer) for peer in sample_peers]:
        copy.wait_recv()
    from_core = send(gram.at[c], gram.at[c], sibling)

    for copy in loss_copies:
        copy.wait_recv()

    halves = [slice(k, min(k + 2 * BLOCK, width)) for k in range(0, width, 2 * BLOCK)]
    returning = []
    for v, g in ((other, c), (c, other)):
        if returning:
            from_core.wait_recv()
        for i in range(n_blocks):
            for j in range(i + 1):
                tile = gram[g, spot(i, j), :]
                full[i * BLOCK : (i + 1) * BLOCK, j * BLOCK : (j + 1) * BLOCK] = tile
                if j < i:
                    flipped = tile.astype(jnp.float32).T.astype(jnp.bfloat16)
                    full[j * BLOCK : (j + 1) * BLOCK, i * BLOCK : (i + 1) * BLOCK] = flipped
        for cs in halves:
            x = norm[v, :, cs]
            product = lax.dot_general(
                full[...], x, (((1,), (0,)), ((), ())), preferred_element_type=jnp.float32
            )
            x = x.astype(jnp.float32)
            grad = (OFF_WEIGHT * inv_rows) * product + extra[:, cs] * norm[g, :, cs].astype(
                jnp.float32
            )
            mean_grad = jnp.sum(grad, axis=0, keepdims=True) * inv_rows
            mean_cross = jnp.sum(grad * x, axis=0, keepdims=True) * inv_rows
            grads[v, :, cs] = (scales[v, :, cs] * (grad - mean_grad - x * mean_cross)).astype(
                jnp.bfloat16
            )
        copies = [
            send(grads.at[v, at(peer[0], rows_dev), :], out.at[v, :, at(s, width)], peer)
            for peer in sample_peers
        ]
        own = pltpu.make_async_copy(
            grads.at[v, at(s, rows_dev), :],
            out.at[v, :, at(s, width)],
            local_sem.at[2 + len(returning)],
        )
        own.start()
        returning.append((copies, own))

    product = jnp.zeros((BLOCK, BLOCK), jnp.float32)
    for i in range(n_blocks):
        for j in range(i + 1):
            pair = gram[0, spot(i, j), :].astype(jnp.float32) * gram[
                1, spot(i, j), :
            ].astype(jnp.float32)
            product = product + (pair if i == j else 2.0 * pair)
    trace = jnp.sum(product, axis=0, keepdims=True) * (OFF_WEIGHT * inv_rows * inv_rows)
    lane_loss = (fold(loss_depth)[0:1, :] + trace) * (1.0 / (cols_dev * blocks))
    loss_out[...] = jnp.broadcast_to(jnp.sum(lane_loss, axis=1, keepdims=True), (8, BLOCK))

    for copies, own in returning:
        own.wait()
        for copy in copies:
            copy.wait_recv()
    for copy in started:
        copy.wait_send()


def body(view_a, view_b):
    rows_dev, cols_dev = view_a.shape
    groups = lax.axis_size("sample")
    blocks = lax.axis_size("feat")
    depth = blocks // CORES
    total_rows = rows_dev * groups
    width = cols_dev // groups
    n_blocks = total_rows // BLOCK
    step = groups * depth * 16
    packed = -(-(n_blocks * (n_blocks + 1) // 2 * BLOCK) // step) * step
    rows_sample = packed // groups
    rows_depth = rows_sample // depth
    copies = 7 * (groups - 1) + 3 * (depth - 1) + 3
    bf16, f32 = jnp.bfloat16, jnp.float32
    vmem = pl.BlockSpec(memory_space=pltpu.VMEM)
    out, loss = pl.pallas_call(
        functools.partial(kernel, groups, blocks),
        out_shape=(
            jax.ShapeDtypeStruct((2, rows_dev, cols_dev), bf16),
            jax.ShapeDtypeStruct((8, BLOCK), f32),
        ),
        in_specs=[vmem, vmem],
        out_specs=(vmem, vmem),
        scratch_shapes=[
            pltpu.VMEM((2, total_rows, width), bf16),
            pltpu.VMEM((2, total_rows, width), bf16),
            pltpu.VMEM((2, 1, width), f32),
            pltpu.VMEM((1, width), f32),
            pltpu.VMEM((packed, BLOCK), f32),
            pltpu.VMEM((packed, BLOCK), bf16),
            pltpu.VMEM((packed, BLOCK), bf16),
            pltpu.VMEM((packed, BLOCK), bf16),
            pltpu.VMEM((groups - 1, rows_sample, BLOCK), bf16),
            pltpu.VMEM((rows_sample, BLOCK), bf16),
            pltpu.VMEM((depth - 1, rows_depth, BLOCK), bf16),
            pltpu.VMEM((2, packed, BLOCK), bf16),
            pltpu.VMEM((total_rows, total_rows), bf16),
            pltpu.VMEM((2, total_rows, width), bf16),
            pltpu.VMEM((CORES, 8, BLOCK), f32),
            pltpu.VMEM((groups, 8, BLOCK), f32),
            pltpu.VMEM((depth, 8, BLOCK), f32),
            pltpu.SemaphoreType.DMA((copies,)),
            pltpu.SemaphoreType.DMA((copies,)),
            pltpu.SemaphoreType.DMA((4,)),
        ],
        compiler_params=pltpu.CompilerParams(
            collective_id=0, has_side_effects=True, vmem_limit_bytes=48 * 1024 * 1024
        ),
    )(view_a, view_b)
    return (loss[0, 0], out[0], out[1])


def solution(mesh):
    in_specs = (P("sample", "feat"), P("sample", "feat"))
    out_specs = (P(), P("sample", "feat"), P("sample", "feat"))
    return jax.shard_map(body, mesh=mesh, in_specs=in_specs, out_specs=out_specs, check_vma=False)
```

```python
import functools

import jax
import jax.numpy as jnp
from jax import lax
from jax.experimental import pallas as pl
from jax.experimental.pallas import tpu as pltpu
from jax.sharding import PartitionSpec as P

EPSILON = 1e-05
OFF_WEIGHT = 0.0051
BLOCK = 128
CORES = 2
MESH = pl.DeviceIdType.MESH


def kernel(
    groups,
    blocks,
    view_a,
    view_b,
    out_a,
    out_b,
    loss_out,
    raw,
    norm,
    scales,
    extra,
    acc,
    send_core,
    recv_core,
    send_sample,
    recv_sample,
    send_depth,
    recv_depth,
    gram,
    full,
    grads,
    loss_core,
    loss_sample,
    loss_depth,
    send_sem,
    recv_sem,
    local_sem,
):
    rows_dev, cols_dev = view_a.shape
    total_rows = rows_dev * groups
    width = cols_dev // groups
    depth = blocks // CORES
    inv_rows = 1.0 / total_rows
    n_blocks = total_rows // BLOCK
    used = n_blocks * (n_blocks + 1) // 2 * BLOCK
    packed = acc.shape[1]
    rows_core = packed // CORES
    rows_sample = rows_core // groups
    rows_depth = rows_sample // depth
    s = lax.axis_index("sample")
    f = lax.axis_index("feat")
    z = lax.div(f, CORES)
    c = lax.rem(f, CORES)
    other = 1 - c
    sample_peers = [(lax.rem(s + d, groups), f) for d in range(1, groups)]
    depth_peers = [(s, lax.rem(z + d, depth) * CORES + c) for d in range(1, depth)]
    sibling = (s, z * CORES + other)
    peers = sample_peers + depth_peers + [sibling]

    barrier = pltpu.get_barrier_semaphore()
    for peer in peers:
        pl.semaphore_signal(barrier, inc=1, device_id=peer, device_id_type=MESH)
    pl.semaphore_wait(barrier, len(peers))

    started = []

    def send(src, dst, peer):
        n = len(started)
        copy = pltpu.make_async_remote_copy(
            src_ref=src,
            dst_ref=dst,
            send_sem=send_sem.at[n],
            recv_sem=recv_sem.at[n],
            device_id=peer,
            device_id_type=MESH,
        )
        copy.start()
        started.append(copy)
        return copy

    def arrived(copies):
        for copy in copies:
            copy.wait_recv()

    def at(index, size):
        return pl.ds(pl.multiple_of(index * size, size), size)

    def send_view(v, view):
        copies = [
            send(view.at[:, at(peer[0], width)], raw.at[v, at(s, rows_dev), :], peer)
            for peer in sample_peers
        ]
        own = pltpu.make_async_copy(
            view.at[:, at(s, width)], raw.at[v, at(s, rows_dev), :], local_sem.at[v]
        )
        own.start()
        return copies, own

    lanes = [slice(k, k + BLOCK) for k in range(0, width, BLOCK)]

    def normalize(v):
        for cs in lanes:
            x = raw[v, :, cs].astype(jnp.float32)
            mean = jnp.sum(x, axis=0, keepdims=True) * inv_rows
            square = jnp.sum(x * x, axis=0, keepdims=True) * inv_rows
            scale = lax.rsqrt(square - mean * mean + EPSILON)
            scales[v, :, cs] = scale
            norm[v, :, cs] = ((x - mean) * scale).astype(jnp.bfloat16)

    def spot(i, j):
        first = (i * (i + 1) // 2 + j) * BLOCK
        return slice(first, first + BLOCK)

    def reduce_core(v):
        if packed > used:
            send_core[v, used:, :] = jnp.zeros((packed - used, BLOCK), jnp.bfloat16)
            acc[v, used:, :] = jnp.zeros((packed - used, BLOCK), jnp.float32)
        for i in range(n_blocks):
            strip = lax.dot_general(
                norm[v, i * BLOCK : (i + 1) * BLOCK, :],
                norm[v, : (i + 1) * BLOCK, :],
                (((1,), (1,)), ((), ())),
                preferred_element_type=jnp.float32,
            )
            for j in range(i + 1):
                tile = strip[:, j * BLOCK : (j + 1) * BLOCK]
                acc[v, spot(i, j), :] = tile
                send_core[v, spot(i, j), :] = tile.astype(jnp.bfloat16)
        return [send(send_core.at[v, at(other, rows_core), :], recv_core.at[v], sibling)]

    def reduce_sample(v):
        mine = at(c, rows_core)
        total = acc[v, mine, :] + recv_core[v].astype(jnp.float32)
        acc[v, mine, :] = total
        send_sample[v] = total.astype(jnp.bfloat16)
        return [
            send(send_sample.at[v, at(peer[0], rows_sample), :], recv_sample.at[v, k], peer)
            for k, peer in enumerate(sample_peers)
        ]

    def reduce_depth(v):
        mine = at(c * groups + s, rows_sample)
        total = acc[v, mine, :]
        for k in range(groups - 1):
            total = total + recv_sample[v, k].astype(jnp.float32)
        acc[v, mine, :] = total
        send_depth[v] = total.astype(jnp.bfloat16)
        return [
            send(
                send_depth.at[v, at(lax.div(peer[1], CORES), rows_depth), :],
                recv_depth.at[v, k],
                peer,
            )
            for k, peer in enumerate(depth_peers)
        ]

    def spread(v, rows, receivers):
        here = gram.at[v, rows, :]
        return [send(here, here, peer) for peer in receivers]

    def gather_depth(v):
        mine = at((c * groups + s) * depth + z, rows_depth)
        total = acc[v, mine, :]
        for k in range(depth - 1):
            total = total + recv_depth[v, k].astype(jnp.float32)
        gram[v, mine, :] = total.astype(jnp.bfloat16)
        return spread(v, mine, depth_peers)

    def gather_sample(v):
        return spread(v, at(c * groups + s, rows_sample), sample_peers)

    def gather_core(v):
        return spread(v, at(c, rows_core), [sibling])

    halves = [slice(k, min(k + 2 * BLOCK, width)) for k in range(0, width, 2 * BLOCK)]

    def return_grad(v, out):
        g = 1 - v
        for i in range(n_blocks):
            for j in range(i + 1):
                tile = gram[g, spot(i, j), :]
                full[i * BLOCK : (i + 1) * BLOCK, j * BLOCK : (j + 1) * BLOCK] = tile
                if j < i:
                    flipped = tile.astype(jnp.float32).T.astype(jnp.bfloat16)
                    full[j * BLOCK : (j + 1) * BLOCK, i * BLOCK : (i + 1) * BLOCK] = flipped
        copies = []
        for cs in halves:
            x = norm[v, :, cs]
            product = lax.dot_general(
                full[...], x, (((1,), (0,)), ((), ())), preferred_element_type=jnp.float32
            )
            x = x.astype(jnp.float32)
            grad = (OFF_WEIGHT * inv_rows) * product + extra[:, cs] * norm[g, :, cs].astype(
                jnp.float32
            )
            mean_grad = jnp.sum(grad, axis=0, keepdims=True) * inv_rows
            mean_cross = jnp.sum(grad * x, axis=0, keepdims=True) * inv_rows
            grads[v, :, cs] = (scales[v, :, cs] * (grad - mean_grad - x * mean_cross)).astype(
                jnp.bfloat16
            )
            size = cs.stop - cs.start
            there = out.at[:, pl.ds(pl.multiple_of(s * width + cs.start, BLOCK), size)]
            copies += [
                send(grads.at[v, at(peer[0], rows_dev), cs], there, peer)
                for peer in sample_peers
            ]
        own = pltpu.make_async_copy(
            grads.at[v, at(s, rows_dev), :], out.at[:, at(s, width)], local_sem.at[2 + v]
        )
        own.start()
        return copies, own

    def fold(slots):
        total = slots[0]
        for k in range(1, slots.shape[0]):
            total = total + slots[k]
        return total

    copies_a, own_a = send_view(0, view_a)
    for copy in copies_a:
        copy.wait_send()
    copies_b, own_b = send_view(1, view_b)
    own_a.wait()
    arrived(copies_a)
    normalize(0)
    step_a = reduce_core(0)
    arrived(step_a)
    step_a = reduce_sample(0)

    own_b.wait()
    arrived(copies_b)
    normalize(1)
    step_b = reduce_core(1)
    part = jnp.zeros((1, BLOCK), jnp.float32)
    for cs in lanes:
        a = norm[0, :, cs].astype(jnp.float32)
        b = norm[1, :, cs].astype(jnp.float32)
        diag = jnp.sum(a * b, axis=0, keepdims=True) * inv_rows
        extra[:, cs] = (1.0 - OFF_WEIGHT) * diag - 1.0
        part = part + (1.0 - diag) * (1.0 - diag) - OFF_WEIGHT * diag * diag
    loss_core[c] = jnp.broadcast_to(part, (8, BLOCK))
    loss_copies = [send(loss_core.at[c], loss_core.at[c], sibling)]

    arrived(step_b)
    step_b = reduce_sample(1)
    arrived(step_a)
    step_a = reduce_depth(0)
    arrived(loss_copies)
    loss_sample[s] = fold(loss_core)
    loss_copies = [send(loss_sample.at[s], loss_sample.at[s], peer) for peer in sample_peers]
    arrived(step_a)
    step_a = gather_depth(0)
    arrived(step_b)
    step_b = reduce_depth(1)
    arrived(loss_copies)
    loss_depth[z] = fold(loss_sample)
    loss_copies = [send(loss_depth.at[z], loss_depth.at[z], peer) for peer in depth_peers]
    arrived(step_a)
    step_a = gather_sample(0)
    arrived(step_b)
    step_b = gather_depth(1)
    arrived(step_a)
    step_a = gather_core(0)
    arrived(step_b)
    step_b = gather_sample(1)
    arrived(step_a)
    returning = [return_grad(1, out_b)]
    arrived(step_b)
    step_b = gather_core(1)
    arrived(step_b)
    returning.append(return_grad(0, out_a))

    arrived(loss_copies)
    product = jnp.zeros((BLOCK, BLOCK), jnp.float32)
    for i in range(n_blocks):
        for j in range(i + 1):
            pair = gram[0, spot(i, j), :].astype(jnp.float32) * gram[
                1, spot(i, j), :
            ].astype(jnp.float32)
            product = product + (pair if i == j else 2.0 * pair)
    trace = jnp.sum(product, axis=0, keepdims=True) * (OFF_WEIGHT * inv_rows * inv_rows)
    lane_loss = (fold(loss_depth)[0:1, :] + trace) * (1.0 / (cols_dev * blocks))
    loss_out[...] = jnp.sum(lane_loss, axis=1, keepdims=True)

    for copies, own in returning:
        own.wait()
        arrived(copies)
    for copy in started[len(copies_a) :]:
        copy.wait_send()


def body(view_a, view_b):
    rows_dev, cols_dev = view_a.shape
    groups = lax.axis_size("sample")
    blocks = lax.axis_size("feat")
    depth = blocks // CORES
    total_rows = rows_dev * groups
    width = cols_dev // groups
    n_blocks = total_rows // BLOCK
    step = CORES * groups * depth * 16
    packed = -(-(n_blocks * (n_blocks + 1) // 2 * BLOCK) // step) * step
    rows_core = packed // CORES
    rows_sample = rows_core // groups
    rows_depth = rows_sample // depth
    halves = -(-width // (2 * BLOCK))
    copies = (2 + 2 + 1 + 2 + 2 * halves) * (groups - 1) + 5 * (depth - 1) + 5
    bf16, f32 = jnp.bfloat16, jnp.float32
    vmem = pl.BlockSpec(memory_space=pltpu.VMEM)
    hbm = pl.BlockSpec(memory_space=pltpu.HBM)
    out_a, out_b, loss = pl.pallas_call(
        functools.partial(kernel, groups, blocks),
        out_shape=(
            jax.ShapeDtypeStruct((rows_dev, cols_dev), bf16),
            jax.ShapeDtypeStruct((rows_dev, cols_dev), bf16),
            jax.ShapeDtypeStruct((1, 1), f32),
        ),
        in_specs=[hbm, hbm],
        out_specs=(hbm, hbm, vmem),
        scratch_shapes=[
            pltpu.VMEM((2, total_rows, width), bf16),
            pltpu.VMEM((2, total_rows, width), bf16),
            pltpu.VMEM((2, 1, width), f32),
            pltpu.VMEM((1, width), f32),
            pltpu.VMEM((2, packed, BLOCK), f32),
            pltpu.VMEM((2, packed, BLOCK), bf16),
            pltpu.VMEM((2, rows_core, BLOCK), bf16),
            pltpu.VMEM((2, rows_core, BLOCK), bf16),
            pltpu.VMEM((2, groups - 1, rows_sample, BLOCK), bf16),
            pltpu.VMEM((2, rows_sample, BLOCK), bf16),
            pltpu.VMEM((2, depth - 1, rows_depth, BLOCK), bf16),
            pltpu.VMEM((2, packed, BLOCK), bf16),
            pltpu.VMEM((total_rows, total_rows), bf16),
            pltpu.VMEM((2, total_rows, width), bf16),
            pltpu.VMEM((CORES, 8, BLOCK), f32),
            pltpu.VMEM((groups, 8, BLOCK), f32),
            pltpu.VMEM((depth, 8, BLOCK), f32),
            pltpu.SemaphoreType.DMA((copies,)),
            pltpu.SemaphoreType.DMA((copies,)),
            pltpu.SemaphoreType.DMA((4,)),
        ],
        compiler_params=pltpu.CompilerParams(
            collective_id=0, has_side_effects=True, vmem_limit_bytes=62 * 1024 * 1024
        ),
    )(view_a, view_b)
    return (loss[0, 0], out_a, out_b)


def solution(mesh):
    in_specs = (P("sample", "feat"), P("sample", "feat"))
    out_specs = (P(), P("sample", "feat"), P("sample", "feat"))
    return jax.shard_map(body, mesh=mesh, in_specs=in_specs, out_specs=out_specs, check_vma=False)
```

```python
import functools

import jax
import jax.numpy as jnp
from jax import lax
from jax.experimental import pallas as pl
from jax.experimental.pallas import tpu as pltpu
from jax.sharding import PartitionSpec as P

EPSILON = 1e-05
OFF_WEIGHT = 0.0051
BLOCK = 128
CORES = 2
MESH = pl.DeviceIdType.MESH


def kernel(
    groups,
    blocks,
    view_a,
    view_b,
    out_a,
    out_b,
    loss_out,
    raw,
    norm,
    scales,
    extra,
    acc,
    send_core,
    recv_core,
    send_sample,
    recv_sample,
    send_depth,
    recv_depth,
    gram,
    full,
    grads,
    products,
    loss_core,
    loss_sample,
    loss_depth,
    send_sem,
    recv_sem,
    local_sem,
):
    rows_dev, cols_dev = view_a.shape
    total_rows = rows_dev * groups
    width = cols_dev // groups
    depth = blocks // CORES
    inv_rows = 1.0 / total_rows
    n_blocks = total_rows // BLOCK
    used = n_blocks * (n_blocks + 1) // 2 * BLOCK
    packed = acc.shape[1]
    rows_core = packed // CORES
    rows_sample = rows_core // groups
    rows_depth = rows_sample // depth
    s = lax.axis_index("sample")
    f = lax.axis_index("feat")
    z = lax.div(f, CORES)
    c = lax.rem(f, CORES)
    other = 1 - c
    sample_peers = [(lax.rem(s + d, groups), f) for d in range(1, groups)]
    depth_peers = [(s, lax.rem(z + d, depth) * CORES + c) for d in range(1, depth)]
    sibling = (s, z * CORES + other)
    peers = sample_peers + depth_peers + [sibling]

    barrier = pltpu.get_barrier_semaphore()
    for peer in peers:
        pl.semaphore_signal(barrier, inc=1, device_id=peer, device_id_type=MESH)
    pl.semaphore_wait(barrier, len(peers))

    started = []

    def send(src, dst, peer):
        n = len(started)
        copy = pltpu.make_async_remote_copy(
            src_ref=src,
            dst_ref=dst,
            send_sem=send_sem.at[n],
            recv_sem=recv_sem.at[n],
            device_id=peer,
            device_id_type=MESH,
        )
        copy.start()
        started.append(copy)
        return copy

    def arrived(copies):
        for copy in copies:
            copy.wait_recv()

    def at(index, size):
        return pl.ds(pl.multiple_of(index * size, size), size)

    def send_view(v, view):
        copies = [
            send(view.at[:, at(peer[0], width)], raw.at[v, at(s, rows_dev), :], peer)
            for peer in sample_peers
        ]
        own = pltpu.make_async_copy(
            view.at[:, at(s, width)], raw.at[v, at(s, rows_dev), :], local_sem.at[v]
        )
        own.start()
        return copies, own

    weight = OFF_WEIGHT * inv_rows
    chunks = [slice(k, k + 64) for k in range(0, total_rows, 64)]

    def octets(x):
        return jnp.sum(x.reshape(x.shape[0] // 8, 8, x.shape[1]), axis=0)

    def normalize(v):
        total = jnp.zeros((8, width), jnp.float32)
        square = jnp.zeros((8, width), jnp.float32)
        for rows in chunks:
            x = raw[v, rows, :].astype(jnp.float32)
            total = total + octets(x)
            square = square + octets(x * x)
        mean = jnp.sum(total, axis=0, keepdims=True) * inv_rows
        square = jnp.sum(square, axis=0, keepdims=True) * inv_rows
        scale = lax.rsqrt(square - mean * mean + EPSILON)
        scales[v] = scale * weight
        for rows in chunks:
            x = raw[v, rows, :].astype(jnp.float32)
            norm[v, rows, :] = ((x - mean) * scale).astype(jnp.bfloat16)

    def spot(i, j):
        first = (i * (i + 1) // 2 + j) * BLOCK
        return slice(first, first + BLOCK)

    def reduce_core(v):
        if packed > used:
            send_core[v, used:, :] = jnp.zeros((packed - used, BLOCK), jnp.bfloat16)
            acc[v, used:, :] = jnp.zeros((packed - used, BLOCK), jnp.float32)
        for first in range(0, n_blocks, 2):
            last = min(first + 2, n_blocks)
            for left in range(0, last, 2):
                right = min(left + 2, last)
                square = lax.dot_general(
                    norm[v, first * BLOCK : last * BLOCK, :],
                    norm[v, left * BLOCK : right * BLOCK, :],
                    (((1,), (1,)), ((), ())),
                    preferred_element_type=jnp.float32,
                )
                for i in range(first, last):
                    for j in range(left, min(right, i + 1)):
                        tile = square[
                            (i - first) * BLOCK : (i - first + 1) * BLOCK,
                            (j - left) * BLOCK : (j - left + 1) * BLOCK,
                        ]
                        acc[v, spot(i, j), :] = tile
                        send_core[v, spot(i, j), :] = tile.astype(jnp.bfloat16)
        return [send(send_core.at[v, at(other, rows_core), :], recv_core.at[v], sibling)]

    def reduce_sample(v):
        mine = at(c, rows_core)
        total = acc[v, mine, :] + recv_core[v].astype(jnp.float32)
        acc[v, mine, :] = total
        send_sample[v] = total.astype(jnp.bfloat16)
        return [
            send(send_sample.at[v, at(peer[0], rows_sample), :], recv_sample.at[v, k], peer)
            for k, peer in enumerate(sample_peers)
        ]

    def reduce_depth(v):
        mine = at(c * groups + s, rows_sample)
        total = acc[v, mine, :]
        for k in range(groups - 1):
            total = total + recv_sample[v, k].astype(jnp.float32)
        acc[v, mine, :] = total
        send_depth[v] = total.astype(jnp.bfloat16)
        return [
            send(
                send_depth.at[v, at(lax.div(peer[1], CORES), rows_depth), :],
                recv_depth.at[v, k],
                peer,
            )
            for k, peer in enumerate(depth_peers)
        ]

    def spread(v, rows, receivers):
        here = gram.at[v, rows, :]
        return [send(here, here, peer) for peer in receivers]

    def gather_depth(v):
        mine = at((c * groups + s) * depth + z, rows_depth)
        total = acc[v, mine, :]
        for k in range(depth - 1):
            total = total + recv_depth[v, k].astype(jnp.float32)
        gram[v, mine, :] = total.astype(jnp.bfloat16)
        return spread(v, mine, depth_peers)

    def gather_sample(v):
        return spread(v, at(c * groups + s, rows_sample), sample_peers)

    def gather_core(v):
        return spread(v, at(c, rows_core), [sibling])

    halves = [slice(k, min(k + 2 * BLOCK, width)) for k in range(0, width, 2 * BLOCK)]

    def return_grad(v, out):
        g = 1 - v
        for i in range(n_blocks):
            for j in range(i + 1):
                tile = gram[g, spot(i, j), :]
                full[i * BLOCK : (i + 1) * BLOCK, j * BLOCK : (j + 1) * BLOCK] = tile
                if j < i:
                    flipped = tile.astype(jnp.float32).T.astype(jnp.bfloat16)
                    full[j * BLOCK : (j + 1) * BLOCK, i * BLOCK : (i + 1) * BLOCK] = flipped
        copies = []
        for cs in halves:
            size = cs.stop - cs.start
            products[:, cs] = lax.dot_general(
                full[...],
                norm[v, :, cs],
                (((1,), (0,)), ((), ())),
                preferred_element_type=jnp.float32,
            )
            mean_grad = jnp.zeros((8, size), jnp.float32)
            mean_cross = jnp.zeros((8, size), jnp.float32)
            for rows in chunks:
                x = norm[v, rows, cs].astype(jnp.float32)
                y = norm[g, rows, cs].astype(jnp.float32)
                grad = products[rows, cs] + extra[:, cs] * y
                products[rows, cs] = grad
                mean_grad = mean_grad + octets(grad)
                mean_cross = mean_cross + octets(grad * x)
            mean_grad = jnp.sum(mean_grad, axis=0, keepdims=True) * inv_rows
            mean_cross = jnp.sum(mean_cross, axis=0, keepdims=True) * inv_rows
            scale = scales[v, :, cs]
            for rows in chunks:
                x = norm[v, rows, cs].astype(jnp.float32)
                grad = products[rows, cs] - mean_grad - x * mean_cross
                grads[v, rows, cs] = (scale * grad).astype(jnp.bfloat16)
            there = out.at[:, pl.ds(pl.multiple_of(s * width + cs.start, BLOCK), size)]
            copies += [
                send(grads.at[v, at(peer[0], rows_dev), cs], there, peer)
                for peer in sample_peers
            ]
        own = pltpu.make_async_copy(
            grads.at[v, at(s, rows_dev), :], out.at[:, at(s, width)], local_sem.at[2 + v]
        )
        own.start()
        return copies, own

    def fold(slots):
        total = slots[0]
        for k in range(1, slots.shape[0]):
            total = total + slots[k]
        return total

    copies_a, own_a = send_view(0, view_a)
    for copy in copies_a:
        copy.wait_send()
    copies_b, own_b = send_view(1, view_b)
    own_a.wait()
    arrived(copies_a)
    normalize(0)
    step_a = reduce_core(0)
    arrived(step_a)
    step_a = reduce_sample(0)

    own_b.wait()
    arrived(copies_b)
    normalize(1)
    step_b = reduce_core(1)
    diag = jnp.zeros((8, width), jnp.float32)
    for rows in chunks:
        x = norm[0, rows, :].astype(jnp.float32) * norm[1, rows, :].astype(jnp.float32)
        diag = diag + octets(x)
    diag = jnp.sum(diag, axis=0, keepdims=True) * inv_rows
    extra[...] = ((1.0 - OFF_WEIGHT) * diag - 1.0) * (1.0 / weight)
    diag = (1.0 - diag) * (1.0 - diag) - OFF_WEIGHT * diag * diag
    part = jnp.zeros((1, BLOCK), jnp.float32)
    for k in range(0, width, BLOCK):
        part = part + diag[:, k : k + BLOCK]
    loss_core[c] = jnp.broadcast_to(part, (8, BLOCK))
    loss_copies = [send(loss_core.at[c], loss_core.at[c], sibling)]

    arrived(step_b)
    step_b = reduce_sample(1)
    arrived(step_a)
    step_a = reduce_depth(0)
    arrived(loss_copies)
    loss_sample[s] = fold(loss_core)
    loss_copies = [send(loss_sample.at[s], loss_sample.at[s], peer) for peer in sample_peers]
    arrived(step_a)
    step_a = gather_depth(0)
    arrived(step_b)
    step_b = reduce_depth(1)
    arrived(loss_copies)
    loss_depth[z] = fold(loss_sample)
    loss_copies = [send(loss_depth.at[z], loss_depth.at[z], peer) for peer in depth_peers]
    arrived(step_a)
    step_a = gather_sample(0)
    arrived(step_b)
    step_b = gather_depth(1)
    arrived(step_a)
    step_a = gather_core(0)
    arrived(step_b)
    step_b = gather_sample(1)
    arrived(step_a)
    returning = [return_grad(1, out_b)]
    arrived(step_b)
    step_b = gather_core(1)
    arrived(step_b)
    returning.append(return_grad(0, out_a))

    arrived(loss_copies)
    product = jnp.zeros((BLOCK, BLOCK), jnp.float32)
    for i in range(n_blocks):
        for j in range(i + 1):
            pair = gram[0, spot(i, j), :].astype(jnp.float32) * gram[
                1, spot(i, j), :
            ].astype(jnp.float32)
            product = product + (pair if i == j else 2.0 * pair)
    trace = jnp.sum(product, axis=0, keepdims=True) * (OFF_WEIGHT * inv_rows * inv_rows)
    lane_loss = (fold(loss_depth)[0:1, :] + trace) * (1.0 / (cols_dev * blocks))
    loss_out[...] = jnp.sum(lane_loss, axis=1, keepdims=True)

    for copies, own in returning:
        own.wait()
        arrived(copies)
    for copy in started[len(copies_a) :]:
        copy.wait_send()


def body(view_a, view_b):
    rows_dev, cols_dev = view_a.shape
    groups = lax.axis_size("sample")
    blocks = lax.axis_size("feat")
    depth = blocks // CORES
    total_rows = rows_dev * groups
    width = cols_dev // groups
    n_blocks = total_rows // BLOCK
    step = CORES * groups * depth * 16
    packed = -(-(n_blocks * (n_blocks + 1) // 2 * BLOCK) // step) * step
    rows_core = packed // CORES
    rows_sample = rows_core // groups
    rows_depth = rows_sample // depth
    halves = -(-width // (2 * BLOCK))
    copies = (2 + 2 + 1 + 2 + 2 * halves) * (groups - 1) + 5 * (depth - 1) + 5
    bf16, f32 = jnp.bfloat16, jnp.float32
    vmem = pl.BlockSpec(memory_space=pltpu.VMEM)
    hbm = pl.BlockSpec(memory_space=pltpu.HBM)
    out_a, out_b, loss = pl.pallas_call(
        functools.partial(kernel, groups, blocks),
        out_shape=(
            jax.ShapeDtypeStruct((rows_dev, cols_dev), bf16),
            jax.ShapeDtypeStruct((rows_dev, cols_dev), bf16),
            jax.ShapeDtypeStruct((1, 1), f32),
        ),
        in_specs=[hbm, hbm],
        out_specs=(vmem, vmem, vmem),
        scratch_shapes=[
            pltpu.VMEM((2, total_rows, width), bf16),
            pltpu.VMEM((2, total_rows, width), bf16),
            pltpu.VMEM((2, 1, width), f32),
            pltpu.VMEM((1, width), f32),
            pltpu.VMEM((2, packed, BLOCK), f32),
            pltpu.VMEM((2, packed, BLOCK), bf16),
            pltpu.VMEM((2, rows_core, BLOCK), bf16),
            pltpu.VMEM((2, rows_core, BLOCK), bf16),
            pltpu.VMEM((2, groups - 1, rows_sample, BLOCK), bf16),
            pltpu.VMEM((2, rows_sample, BLOCK), bf16),
            pltpu.VMEM((2, depth - 1, rows_depth, BLOCK), bf16),
            pltpu.VMEM((2, packed, BLOCK), bf16),
            pltpu.VMEM((total_rows, total_rows), bf16),
            pltpu.VMEM((2, total_rows, width), bf16),
            pltpu.VMEM((total_rows, width), f32),
            pltpu.VMEM((CORES, 8, BLOCK), f32),
            pltpu.VMEM((groups, 8, BLOCK), f32),
            pltpu.VMEM((depth, 8, BLOCK), f32),
            pltpu.SemaphoreType.DMA((copies,)),
            pltpu.SemaphoreType.DMA((copies,)),
            pltpu.SemaphoreType.DMA((4,)),
        ],
        compiler_params=pltpu.CompilerParams(
            collective_id=0, has_side_effects=True, vmem_limit_bytes=48 * 1024 * 1024
        ),
    )(
        pltpu.with_memory_space_constraint(view_a, pltpu.HBM),
        pltpu.with_memory_space_constraint(view_b, pltpu.HBM),
    )
    return (loss[0, 0], out_a, out_b)


def solution(mesh):
    in_specs = (P("sample", "feat"), P("sample", "feat"))
    out_specs = (P(), P("sample", "feat"), P("sample", "feat"))
    return jax.shard_map(body, mesh=mesh, in_specs=in_specs, out_specs=out_specs, check_vma=False)
```

```python
import functools

import jax
import jax.numpy as jnp
from jax import lax
from jax.experimental import pallas as pl
from jax.experimental.pallas import tpu as pltpu
from jax.sharding import PartitionSpec as P

EPSILON = 1e-05
OFF_WEIGHT = 0.0051
BLOCK = 128
CORES = 2
MESH = pl.DeviceIdType.MESH


def kernel(
    groups,
    blocks,
    view_a,
    view_b,
    out_a,
    out_b,
    loss_out,
    raw,
    norm,
    scales,
    extra,
    acc,
    send_core,
    recv_core,
    send_sample,
    recv_sample,
    send_depth,
    recv_depth,
    gram,
    full,
    grads,
    products,
    loss_core,
    loss_sample,
    loss_depth,
    send_sem,
    recv_sem,
    local_sem,
):
    rows_dev, cols_dev = view_a.shape
    total_rows = rows_dev * groups
    width = cols_dev // groups
    depth = blocks // CORES
    inv_rows = 1.0 / total_rows
    n_blocks = total_rows // BLOCK
    used = n_blocks * (n_blocks + 1) // 2 * BLOCK
    packed = acc.shape[1]
    rows_core = packed // CORES
    rows_sample = rows_core // groups
    rows_depth = rows_sample // depth
    s = lax.axis_index("sample")
    f = lax.axis_index("feat")
    z = lax.div(f, CORES)
    c = lax.rem(f, CORES)
    other = 1 - c
    sample_peers = [(lax.rem(s + d, groups), f) for d in range(1, groups)]
    depth_peers = [(s, lax.rem(z + d, depth) * CORES + c) for d in range(1, depth)]
    sibling = (s, z * CORES + other)
    peers = sample_peers + depth_peers + [sibling]

    barrier = pltpu.get_barrier_semaphore()
    for peer in peers:
        pl.semaphore_signal(barrier, inc=1, device_id=peer, device_id_type=MESH)
    pl.semaphore_wait(barrier, len(peers))

    started = []

    def send(src, dst, peer):
        n = len(started)
        copy = pltpu.make_async_remote_copy(
            src_ref=src,
            dst_ref=dst,
            send_sem=send_sem.at[n],
            recv_sem=recv_sem.at[n],
            device_id=peer,
            device_id_type=MESH,
        )
        copy.start()
        started.append(copy)
        return copy

    def arrived(copies):
        for copy in copies:
            copy.wait_recv()

    def at(index, size):
        return pl.ds(pl.multiple_of(index * size, size), size)

    def send_view(v, view):
        copies = [
            send(view.at[:, at(peer[0], width)], raw.at[v, at(s, rows_dev), :], peer)
            for peer in sample_peers
        ]
        own = pltpu.make_async_copy(
            view.at[:, at(s, width)], raw.at[v, at(s, rows_dev), :], local_sem.at[v]
        )
        own.start()
        return copies, own

    weight = OFF_WEIGHT * inv_rows
    chunks = [slice(k, k + 64) for k in range(0, total_rows, 64)]

    def octets(x):
        return jnp.sum(x.reshape(x.shape[0] // 8, 8, x.shape[1]), axis=0)

    def normalize(v):
        total = jnp.zeros((8, width), jnp.float32)
        square = jnp.zeros((8, width), jnp.float32)
        for rows in chunks:
            x = raw[v, rows, :].astype(jnp.float32)
            total = total + octets(x)
            square = square + octets(x * x)
        mean = jnp.sum(total, axis=0, keepdims=True) * inv_rows
        square = jnp.sum(square, axis=0, keepdims=True) * inv_rows
        scale = lax.rsqrt(square - mean * mean + EPSILON)
        scales[v] = scale * weight
        for rows in chunks:
            x = raw[v, rows, :].astype(jnp.float32)
            norm[v, rows, :] = ((x - mean) * scale).astype(jnp.bfloat16)

    def spot(i, j):
        first = (i * (i + 1) // 2 + j) * BLOCK
        return slice(first, first + BLOCK)

    def reduce_core(v):
        if packed > used:
            send_core[v, used:, :] = jnp.zeros((packed - used, BLOCK), jnp.bfloat16)
            acc[v, used:, :] = jnp.zeros((packed - used, BLOCK), jnp.float32)
        for first in range(0, n_blocks, 2):
            last = min(first + 2, n_blocks)
            for left in range(0, last, 2):
                right = min(left + 2, last)
                square = lax.dot_general(
                    norm[v, first * BLOCK : last * BLOCK, :],
                    norm[v, left * BLOCK : right * BLOCK, :],
                    (((1,), (1,)), ((), ())),
                    preferred_element_type=jnp.float32,
                )
                for i in range(first, last):
                    for j in range(left, min(right, i + 1)):
                        tile = square[
                            (i - first) * BLOCK : (i - first + 1) * BLOCK,
                            (j - left) * BLOCK : (j - left + 1) * BLOCK,
                        ]
                        acc[v, spot(i, j), :] = tile
                        send_core[v, spot(i, j), :] = tile.astype(jnp.bfloat16)
        return [send(send_core.at[v, at(other, rows_core), :], recv_core.at[v], sibling)]

    def reduce_sample(v):
        mine = at(c, rows_core)
        total = acc[v, mine, :] + recv_core[v].astype(jnp.float32)
        acc[v, mine, :] = total
        send_sample[v] = total.astype(jnp.bfloat16)
        return [
            send(send_sample.at[v, at(peer[0], rows_sample), :], recv_sample.at[v, k], peer)
            for k, peer in enumerate(sample_peers)
        ]

    def reduce_depth(v):
        mine = at(c * groups + s, rows_sample)
        total = acc[v, mine, :]
        for k in range(groups - 1):
            total = total + recv_sample[v, k].astype(jnp.float32)
        acc[v, mine, :] = total
        send_depth[v] = total.astype(jnp.bfloat16)
        return [
            send(
                send_depth.at[v, at(lax.div(peer[1], CORES), rows_depth), :],
                recv_depth.at[v, k],
                peer,
            )
            for k, peer in enumerate(depth_peers)
        ]

    def spread(v, rows, receivers):
        here = gram.at[v, rows, :]
        return [send(here, here, peer) for peer in receivers]

    def gather_depth(v):
        mine = at((c * groups + s) * depth + z, rows_depth)
        total = acc[v, mine, :]
        for k in range(depth - 1):
            total = total + recv_depth[v, k].astype(jnp.float32)
        gram[v, mine, :] = total.astype(jnp.bfloat16)
        return spread(v, mine, depth_peers)

    def gather_sample(v):
        return spread(v, at(c * groups + s, rows_sample), sample_peers)

    def gather_core(v):
        return spread(v, at(c, rows_core), [sibling])

    halves = [slice(k, min(k + 2 * BLOCK, width)) for k in range(0, width, 2 * BLOCK)]

    def return_half(v, out, cs):
        first = pl.multiple_of(s * width + cs.start, BLOCK)
        there = out.at[:, pl.ds(first, cs.stop - cs.start)]
        return [
            send(grads.at[v, at(peer[0], rows_dev), cs], there, peer) for peer in sample_peers
        ]

    def make_grad(v, out, finish):
        g = 1 - v
        for i in range(n_blocks):
            for j in range(i + 1):
                tile = gram[g, spot(i, j), :]
                full[i * BLOCK : (i + 1) * BLOCK, j * BLOCK : (j + 1) * BLOCK] = tile
                if j < i:
                    flipped = tile.astype(jnp.float32).T.astype(jnp.bfloat16)
                    full[j * BLOCK : (j + 1) * BLOCK, i * BLOCK : (i + 1) * BLOCK] = flipped
        copies = []
        for cs in halves:
            size = cs.stop - cs.start
            products[:, cs] = lax.dot_general(
                full[...],
                norm[v, :, cs],
                (((1,), (0,)), ((), ())),
                preferred_element_type=jnp.float32,
            )
            mean_grad = jnp.zeros((8, size), jnp.float32)
            mean_cross = jnp.zeros((8, size), jnp.float32)
            for rows in chunks:
                x = norm[v, rows, cs].astype(jnp.float32)
                y = norm[g, rows, cs].astype(jnp.float32)
                grad = products[rows, cs] + extra[:, cs] * y
                products[rows, cs] = grad
                mean_grad = mean_grad + octets(grad)
                mean_cross = mean_cross + octets(grad * x)
            mean_grad = jnp.sum(mean_grad, axis=0, keepdims=True) * inv_rows
            mean_cross = jnp.sum(mean_cross, axis=0, keepdims=True) * inv_rows
            scale = scales[v, :, cs]
            for rows in chunks:
                x = norm[v, rows, cs].astype(jnp.float32)
                grad = products[rows, cs] - mean_grad - x * mean_cross
                grads[v, rows, cs] = (scale * grad).astype(jnp.bfloat16)
            if finish is None:
                copies += return_half(v, out, cs)
        if finish is not None:
            finish()
            for cs in halves:
                copies += return_half(v, out, cs)
        own = pltpu.make_async_copy(
            grads.at[v, at(s, rows_dev), :], out.at[:, at(s, width)], local_sem.at[2 + v]
        )
        own.start()
        return copies, own

    def fold(slots):
        total = slots[0]
        for k in range(1, slots.shape[0]):
            total = total + slots[k]
        return total

    copies_a, own_a = send_view(0, view_a)
    for copy in copies_a:
        copy.wait_send()
    copies_b, own_b = send_view(1, view_b)
    own_a.wait()
    arrived(copies_a)
    normalize(0)
    step_a = reduce_core(0)
    arrived(step_a)
    step_a = reduce_sample(0)
    arrived(step_a)
    step_a = reduce_depth(0)

    own_b.wait()
    arrived(copies_b)
    normalize(1)
    step_b = reduce_core(1)
    diag = jnp.zeros((8, width), jnp.float32)
    for rows in chunks:
        x = norm[0, rows, :].astype(jnp.float32) * norm[1, rows, :].astype(jnp.float32)
        diag = diag + octets(x)
    diag = jnp.sum(diag, axis=0, keepdims=True) * inv_rows
    extra[...] = ((1.0 - OFF_WEIGHT) * diag - 1.0) * (1.0 / weight)
    diag = (1.0 - diag) * (1.0 - diag) - OFF_WEIGHT * diag * diag
    part = jnp.zeros((1, BLOCK), jnp.float32)
    for k in range(0, width, BLOCK):
        part = part + diag[:, k : k + BLOCK]
    loss_core[c] = jnp.broadcast_to(part, (8, BLOCK))
    loss_copies = [send(loss_core.at[c], loss_core.at[c], sibling)]

    arrived(step_b)
    step_b = reduce_sample(1)
    arrived(step_a)
    step_a = gather_depth(0)
    arrived(loss_copies)
    loss_sample[s] = fold(loss_core)
    loss_copies = [send(loss_sample.at[s], loss_sample.at[s], peer) for peer in sample_peers]
    arrived(step_b)
    step_b = reduce_depth(1)
    arrived(step_a)
    step_a = gather_sample(0)
    arrived(loss_copies)
    loss_depth[z] = fold(loss_sample)
    loss_copies = [send(loss_depth.at[z], loss_depth.at[z], peer) for peer in depth_peers]
    arrived(step_b)
    step_b = gather_depth(1)
    arrived(step_a)
    step_a = gather_core(0)
    arrived(step_b)
    step_b = gather_sample(1)
    arrived(step_a)
    step_a = []

    def finish():
        arrived(step_b)
        step_a.extend(gather_core(1))

    returning = [make_grad(1, out_b, finish)]
    arrived(step_a)
    returning.append(make_grad(0, out_a, None))

    arrived(loss_copies)
    product = jnp.zeros((BLOCK, BLOCK), jnp.float32)
    for i in range(n_blocks):
        for j in range(i + 1):
            pair = gram[0, spot(i, j), :].astype(jnp.float32) * gram[
                1, spot(i, j), :
            ].astype(jnp.float32)
            product = product + (pair if i == j else 2.0 * pair)
    trace = jnp.sum(product, axis=0, keepdims=True) * (OFF_WEIGHT * inv_rows * inv_rows)
    lane_loss = (fold(loss_depth)[0:1, :] + trace) * (1.0 / (cols_dev * blocks))
    loss_out[...] = jnp.sum(lane_loss, axis=1, keepdims=True)

    for copies, own in returning:
        own.wait()
        arrived(copies)
    for copy in started[len(copies_a) :]:
        copy.wait_send()


def body(view_a, view_b):
    rows_dev, cols_dev = view_a.shape
    groups = lax.axis_size("sample")
    blocks = lax.axis_size("feat")
    depth = blocks // CORES
    total_rows = rows_dev * groups
    width = cols_dev // groups
    n_blocks = total_rows // BLOCK
    step = CORES * groups * depth * 16
    packed = -(-(n_blocks * (n_blocks + 1) // 2 * BLOCK) // step) * step
    rows_core = packed // CORES
    rows_sample = rows_core // groups
    rows_depth = rows_sample // depth
    halves = -(-width // (2 * BLOCK))
    copies = (2 + 2 + 1 + 2 + 2 * halves) * (groups - 1) + 5 * (depth - 1) + 5
    bf16, f32 = jnp.bfloat16, jnp.float32
    vmem = pl.BlockSpec(memory_space=pltpu.VMEM)
    hbm = pl.BlockSpec(memory_space=pltpu.HBM)
    out_a, out_b, loss = pl.pallas_call(
        functools.partial(kernel, groups, blocks),
        out_shape=(
            jax.ShapeDtypeStruct((rows_dev, cols_dev), bf16),
            jax.ShapeDtypeStruct((rows_dev, cols_dev), bf16),
            jax.ShapeDtypeStruct((1, 1), f32),
        ),
        in_specs=[hbm, hbm],
        out_specs=(vmem, vmem, vmem),
        scratch_shapes=[
            pltpu.VMEM((2, total_rows, width), bf16),
            pltpu.VMEM((2, total_rows, width), bf16),
            pltpu.VMEM((2, 1, width), f32),
            pltpu.VMEM((1, width), f32),
            pltpu.VMEM((2, packed, BLOCK), f32),
            pltpu.VMEM((2, packed, BLOCK), bf16),
            pltpu.VMEM((2, rows_core, BLOCK), bf16),
            pltpu.VMEM((2, rows_core, BLOCK), bf16),
            pltpu.VMEM((2, groups - 1, rows_sample, BLOCK), bf16),
            pltpu.VMEM((2, rows_sample, BLOCK), bf16),
            pltpu.VMEM((2, depth - 1, rows_depth, BLOCK), bf16),
            pltpu.VMEM((2, packed, BLOCK), bf16),
            pltpu.VMEM((total_rows, total_rows), bf16),
            pltpu.VMEM((2, total_rows, width), bf16),
            pltpu.VMEM((total_rows, width), f32),
            pltpu.VMEM((CORES, 8, BLOCK), f32),
            pltpu.VMEM((groups, 8, BLOCK), f32),
            pltpu.VMEM((depth, 8, BLOCK), f32),
            pltpu.SemaphoreType.DMA((copies,)),
            pltpu.SemaphoreType.DMA((copies,)),
            pltpu.SemaphoreType.DMA((4,)),
        ],
        compiler_params=pltpu.CompilerParams(
            collective_id=0, has_side_effects=True, vmem_limit_bytes=48 * 1024 * 1024
        ),
    )(
        pltpu.with_memory_space_constraint(view_a, pltpu.HBM),
        pltpu.with_memory_space_constraint(view_b, pltpu.HBM),
    )
    return (loss[0, 0], out_a, out_b)


def solution(mesh):
    in_specs = (P("sample", "feat"), P("sample", "feat"))
    out_specs = (P(), P("sample", "feat"), P("sample", "feat"))
    return jax.shard_map(body, mesh=mesh, in_specs=in_specs, out_specs=out_specs, check_vma=False)
```

```python
import functools

import jax
import jax.numpy as jnp
from jax import lax
from jax.experimental import pallas as pl
from jax.experimental.pallas import tpu as pltpu
from jax.sharding import PartitionSpec as P

EPSILON = 1e-05
OFF_WEIGHT = 0.0051
BLOCK = 128
CORES = 2
HIGH = 2
MESH = pl.DeviceIdType.MESH


def kernel(
    groups,
    blocks,
    view_a,
    view_b,
    out_a,
    out_b,
    loss_out,
    raw,
    norm,
    scales,
    extra,
    acc,
    send_core,
    recv_core,
    send_sample,
    recv_sample,
    send_depth,
    recv_depth,
    relay_in,
    relay_out,
    gram,
    full,
    grads,
    products,
    loss_core,
    loss_sample,
    loss_depth,
    send_sem,
    recv_sem,
    local_sem,
):
    rows_dev, cols_dev = view_a.shape
    total_rows = rows_dev * groups
    width = cols_dev // groups
    depth = blocks // CORES
    inv_rows = 1.0 / total_rows
    n_blocks = total_rows // BLOCK
    used = n_blocks * (n_blocks + 1) // 2 * BLOCK
    packed = acc.shape[1]
    rows_core = packed // CORES
    rows_sample = rows_core // groups
    rows_depth = rows_sample // depth
    s = lax.axis_index("sample")
    f = lax.axis_index("feat")
    z = lax.div(f, CORES)
    c = lax.rem(f, CORES)
    other = 1 - c
    sample_peers = [(lax.rem(s + d, groups), f) for d in range(1, groups)]
    depth_peers = [(s, lax.rem(z + d, depth) * CORES + c) for d in range(1, depth)]
    sibling = (s, z * CORES + other)
    peers = sample_peers + depth_peers + [sibling]

    barrier = pltpu.get_barrier_semaphore()
    for peer in peers:
        pl.semaphore_signal(barrier, inc=1, device_id=peer, device_id_type=MESH)
    pl.semaphore_wait(barrier, len(peers))

    started = []

    def send(src, dst, peer):
        n = len(started)
        copy = pltpu.make_async_remote_copy(
            src_ref=src,
            dst_ref=dst,
            send_sem=send_sem.at[n],
            recv_sem=recv_sem.at[n],
            device_id=peer,
            device_id_type=MESH,
        )
        copy.start()
        started.append(copy)
        return copy

    def arrived(copies):
        for copy in copies:
            copy.wait_recv()

    def at(index, size):
        return pl.ds(pl.multiple_of(index * size, size), size)

    low = groups // HIGH
    hi, lo = lax.div(s, low), lax.rem(s, low)
    half_rows = rows_dev // 2
    whole, first_half, second_half = (
        pl.ds(0, rows_dev),
        pl.ds(0, half_rows),
        pl.ds(half_rows, half_rows),
    )

    def there(dh, dl):
        return lax.rem(hi + dh + HIGH, HIGH) * low + lax.rem(lo + dl + low, low)

    def exchange(source, target, relay):
        first_hop = []
        for dh in range(1, HIGH):
            for dl in range(1, low):
                k = (dh - 1) * (low - 1) + dl - 1
                to = there(dh, dl)
                for way, rows, via in (
                    (0, first_half, there(0, dl)),
                    (1, second_half, there(dh, 0)),
                ):
                    copy = send(source(to, rows), relay.at[way, k], (via, f))
                    first_hop.append((copy, way, k, dh, dl))
        direct = [(0, dl) for dl in range(1, low)] + [(dh, 0) for dh in range(1, HIGH)]
        copies = [
            send(source(there(*d), whole), target(s, whole), (there(*d), f)) for d in direct
        ]

        def forward():
            for copy, way, k, dh, dl in first_hop:
                copy.wait_recv()
                if way == 0:
                    origin, rows, to = there(0, -dl), first_half, there(dh, 0)
                else:
                    origin, rows, to = there(-dh, 0), second_half, there(0, dl)
                copies.append(send(relay.at[way, k], target(origin, rows), (to, f)))

        return copies, forward

    def send_view(v, view):
        def source(p, rows):
            return view.at[rows, at(p, width)]

        def target(p, rows):
            first = pl.multiple_of(p * rows_dev + rows.start, half_rows)
            return raw.at[v, pl.ds(first, rows.size), :]

        copies = exchange(source, target, relay_in.at[v])
        own = pltpu.make_async_copy(
            view.at[:, at(s, width)], raw.at[v, at(s, rows_dev), :], local_sem.at[v]
        )
        own.start()
        return copies[0], copies[1], own

    weight = OFF_WEIGHT * inv_rows
    chunks = [slice(k, k + 64) for k in range(0, total_rows, 64)]

    def octets(x):
        return jnp.sum(x.reshape(x.shape[0] // 8, 8, x.shape[1]), axis=0)

    def normalize(v):
        total = jnp.zeros((8, width), jnp.float32)
        square = jnp.zeros((8, width), jnp.float32)
        for rows in chunks:
            x = raw[v, rows, :].astype(jnp.float32)
            total = total + octets(x)
            square = square + octets(x * x)
        mean = jnp.sum(total, axis=0, keepdims=True) * inv_rows
        square = jnp.sum(square, axis=0, keepdims=True) * inv_rows
        scale = lax.rsqrt(square - mean * mean + EPSILON)
        scales[v] = scale * weight
        for rows in chunks:
            x = raw[v, rows, :].astype(jnp.float32)
            norm[v, rows, :] = ((x - mean) * scale).astype(jnp.bfloat16)

    def spot(i, j):
        first = (i * (i + 1) // 2 + j) * BLOCK
        return slice(first, first + BLOCK)

    def reduce_core(v):
        if packed > used:
            send_core[v, used:, :] = jnp.zeros((packed - used, BLOCK), jnp.bfloat16)
            acc[v, used:, :] = jnp.zeros((packed - used, BLOCK), jnp.float32)
        for first in range(0, n_blocks, 2):
            last = min(first + 2, n_blocks)
            for left in range(0, last, 2):
                right = min(left + 2, last)
                square = lax.dot_general(
                    norm[v, first * BLOCK : last * BLOCK, :],
                    norm[v, left * BLOCK : right * BLOCK, :],
                    (((1,), (1,)), ((), ())),
                    preferred_element_type=jnp.float32,
                )
                for i in range(first, last):
                    for j in range(left, min(right, i + 1)):
                        tile = square[
                            (i - first) * BLOCK : (i - first + 1) * BLOCK,
                            (j - left) * BLOCK : (j - left + 1) * BLOCK,
                        ]
                        acc[v, spot(i, j), :] = tile
                        send_core[v, spot(i, j), :] = tile.astype(jnp.bfloat16)
        return [send(send_core.at[v, at(other, rows_core), :], recv_core.at[v], sibling)]

    def reduce_sample(v):
        mine = at(c, rows_core)
        total = acc[v, mine, :] + recv_core[v].astype(jnp.float32)
        acc[v, mine, :] = total
        send_sample[v] = total.astype(jnp.bfloat16)
        return [
            send(send_sample.at[v, at(peer[0], rows_sample), :], recv_sample.at[v, k], peer)
            for k, peer in enumerate(sample_peers)
        ]

    def reduce_depth(v):
        mine = at(c * groups + s, rows_sample)
        total = acc[v, mine, :]
        for k in range(groups - 1):
            total = total + recv_sample[v, k].astype(jnp.float32)
        acc[v, mine, :] = total
        send_depth[v] = total.astype(jnp.bfloat16)
        return [
            send(
                send_depth.at[v, at(lax.div(peer[1], CORES), rows_depth), :],
                recv_depth.at[v, k],
                peer,
            )
            for k, peer in enumerate(depth_peers)
        ]

    def spread(v, rows, receivers):
        here = gram.at[v, rows, :]
        return [send(here, here, peer) for peer in receivers]

    def gather_depth(v):
        mine = at((c * groups + s) * depth + z, rows_depth)
        total = acc[v, mine, :]
        for k in range(depth - 1):
            total = total + recv_depth[v, k].astype(jnp.float32)
        gram[v, mine, :] = total.astype(jnp.bfloat16)
        return spread(v, mine, depth_peers)

    def gather_sample(v):
        return spread(v, at(c * groups + s, rows_sample), sample_peers)

    def gather_core(v):
        return spread(v, at(c, rows_core), [sibling])

    halves = [slice(k, min(k + 2 * BLOCK, width)) for k in range(0, width, 2 * BLOCK)]

    def return_grad(v, out):
        g = 1 - v
        for i in range(n_blocks):
            for j in range(i + 1):
                tile = gram[g, spot(i, j), :]
                full[i * BLOCK : (i + 1) * BLOCK, j * BLOCK : (j + 1) * BLOCK] = tile
                if j < i:
                    flipped = tile.astype(jnp.float32).T.astype(jnp.bfloat16)
                    full[j * BLOCK : (j + 1) * BLOCK, i * BLOCK : (i + 1) * BLOCK] = flipped
        for cs in halves:
            size = cs.stop - cs.start
            products[:, cs] = lax.dot_general(
                full[...],
                norm[v, :, cs],
                (((1,), (0,)), ((), ())),
                preferred_element_type=jnp.float32,
            )
            mean_grad = jnp.zeros((8, size), jnp.float32)
            mean_cross = jnp.zeros((8, size), jnp.float32)
            for rows in chunks:
                x = norm[v, rows, cs].astype(jnp.float32)
                y = norm[g, rows, cs].astype(jnp.float32)
                grad = products[rows, cs] + extra[:, cs] * y
                products[rows, cs] = grad
                mean_grad = mean_grad + octets(grad)
                mean_cross = mean_cross + octets(grad * x)
            mean_grad = jnp.sum(mean_grad, axis=0, keepdims=True) * inv_rows
            mean_cross = jnp.sum(mean_cross, axis=0, keepdims=True) * inv_rows
            scale = scales[v, :, cs]
            for rows in chunks:
                x = norm[v, rows, cs].astype(jnp.float32)
                grad = products[rows, cs] - mean_grad - x * mean_cross
                grads[v, rows, cs] = (scale * grad).astype(jnp.bfloat16)

        def source(p, rows):
            first = pl.multiple_of(p * rows_dev + rows.start, half_rows)
            return grads.at[v, pl.ds(first, rows.size), :]

        def target(p, rows):
            return out.at[rows, at(p, width)]

        copies, forward = exchange(source, target, relay_out.at[v])
        own = pltpu.make_async_copy(
            grads.at[v, at(s, rows_dev), :], out.at[:, at(s, width)], local_sem.at[2 + v]
        )
        own.start()
        return copies, forward, own

    def fold(slots):
        total = slots[0]
        for k in range(1, slots.shape[0]):
            total = total + slots[k]
        return total

    copies_a, forward_a, own_a = send_view(0, view_a)
    forward_a()
    copies_b, forward_b, own_b = send_view(1, view_b)
    own_a.wait()
    arrived(copies_a)
    normalize(0)
    step_a = reduce_core(0)
    forward_b()
    arrived(step_a)
    step_a = reduce_sample(0)

    own_b.wait()
    arrived(copies_b)
    normalize(1)
    step_b = reduce_core(1)
    diag = jnp.zeros((8, width), jnp.float32)
    for rows in chunks:
        x = norm[0, rows, :].astype(jnp.float32) * norm[1, rows, :].astype(jnp.float32)
        diag = diag + octets(x)
    diag = jnp.sum(diag, axis=0, keepdims=True) * inv_rows
    extra[...] = ((1.0 - OFF_WEIGHT) * diag - 1.0) * (1.0 / weight)
    diag = (1.0 - diag) * (1.0 - diag) - OFF_WEIGHT * diag * diag
    part = jnp.zeros((1, BLOCK), jnp.float32)
    for k in range(0, width, BLOCK):
        part = part + diag[:, k : k + BLOCK]
    loss_core[c] = jnp.broadcast_to(part, (8, BLOCK))
    loss_copies = [send(loss_core.at[c], loss_core.at[c], sibling)]

    arrived(step_b)
    step_b = reduce_sample(1)
    arrived(step_a)
    step_a = reduce_depth(0)
    arrived(loss_copies)
    loss_sample[s] = fold(loss_core)
    loss_copies = [send(loss_sample.at[s], loss_sample.at[s], peer) for peer in sample_peers]
    arrived(step_a)
    step_a = gather_depth(0)
    arrived(step_b)
    step_b = reduce_depth(1)
    arrived(loss_copies)
    loss_depth[z] = fold(loss_sample)
    loss_copies = [send(loss_depth.at[z], loss_depth.at[z], peer) for peer in depth_peers]
    arrived(step_a)
    step_a = gather_sample(0)
    arrived(step_b)
    step_b = gather_depth(1)
    arrived(step_a)
    step_a = gather_core(0)
    arrived(step_b)
    step_b = gather_sample(1)
    arrived(step_a)
    returning = [return_grad(1, out_b)]
    arrived(step_b)
    step_b = gather_core(1)
    returning[0][1]()
    arrived(step_b)
    returning.append(return_grad(0, out_a))
    returning[1][1]()

    arrived(loss_copies)
    product = jnp.zeros((BLOCK, BLOCK), jnp.float32)
    for i in range(n_blocks):
        for j in range(i + 1):
            pair = gram[0, spot(i, j), :].astype(jnp.float32) * gram[
                1, spot(i, j), :
            ].astype(jnp.float32)
            product = product + (pair if i == j else 2.0 * pair)
    trace = jnp.sum(product, axis=0, keepdims=True) * (OFF_WEIGHT * inv_rows * inv_rows)
    lane_loss = (fold(loss_depth)[0:1, :] + trace) * (1.0 / (cols_dev * blocks))
    loss_out[...] = jnp.sum(lane_loss, axis=1, keepdims=True)

    for copies, _, own in returning:
        own.wait()
        arrived(copies)
    for copy in started:
        copy.wait_send()


def body(view_a, view_b):
    rows_dev, cols_dev = view_a.shape
    groups = lax.axis_size("sample")
    blocks = lax.axis_size("feat")
    depth = blocks // CORES
    total_rows = rows_dev * groups
    width = cols_dev // groups
    n_blocks = total_rows // BLOCK
    step = CORES * groups * depth * 16
    packed = -(-(n_blocks * (n_blocks + 1) // 2 * BLOCK) // step) * step
    rows_core = packed // CORES
    rows_sample = rows_core // groups
    rows_depth = rows_sample // depth
    low = groups // HIGH
    pairs = (HIGH - 1) * (low - 1)
    relay = (2, 2, pairs, rows_dev // 2, width)
    exchanged = 4 * pairs + low - 1 + HIGH - 1
    copies = 4 * exchanged + 3 * (groups - 1) + 2 * (groups - 1) + 5 * (depth - 1) + 5
    bf16, f32 = jnp.bfloat16, jnp.float32
    vmem = pl.BlockSpec(memory_space=pltpu.VMEM)
    hbm = pl.BlockSpec(memory_space=pltpu.HBM)
    out_a, out_b, loss = pl.pallas_call(
        functools.partial(kernel, groups, blocks),
        out_shape=(
            jax.ShapeDtypeStruct((rows_dev, cols_dev), bf16),
            jax.ShapeDtypeStruct((rows_dev, cols_dev), bf16),
            jax.ShapeDtypeStruct((1, 1), f32),
        ),
        in_specs=[hbm, hbm],
        out_specs=(vmem, vmem, vmem),
        scratch_shapes=[
            pltpu.VMEM((2, total_rows, width), bf16),
            pltpu.VMEM((2, total_rows, width), bf16),
            pltpu.VMEM((2, 1, width), f32),
            pltpu.VMEM((1, width), f32),
            pltpu.VMEM((2, packed, BLOCK), f32),
            pltpu.VMEM((2, packed, BLOCK), bf16),
            pltpu.VMEM((2, rows_core, BLOCK), bf16),
            pltpu.VMEM((2, rows_core, BLOCK), bf16),
            pltpu.VMEM((2, groups - 1, rows_sample, BLOCK), bf16),
            pltpu.VMEM((2, rows_sample, BLOCK), bf16),
            pltpu.VMEM((2, depth - 1, rows_depth, BLOCK), bf16),
            pltpu.VMEM(relay, bf16),
            pltpu.VMEM(relay, bf16),
            pltpu.VMEM((2, packed, BLOCK), bf16),
            pltpu.VMEM((total_rows, total_rows), bf16),
            pltpu.VMEM((2, total_rows, width), bf16),
            pltpu.VMEM((total_rows, width), f32),
            pltpu.VMEM((CORES, 8, BLOCK), f32),
            pltpu.VMEM((groups, 8, BLOCK), f32),
            pltpu.VMEM((depth, 8, BLOCK), f32),
            pltpu.SemaphoreType.DMA((copies,)),
            pltpu.SemaphoreType.DMA((copies,)),
            pltpu.SemaphoreType.DMA((4,)),
        ],
        compiler_params=pltpu.CompilerParams(
            collective_id=0, has_side_effects=True, vmem_limit_bytes=48 * 1024 * 1024
        ),
    )(
        pltpu.with_memory_space_constraint(view_a, pltpu.HBM),
        pltpu.with_memory_space_constraint(view_b, pltpu.HBM),
    )
    return (loss[0, 0], out_a, out_b)


def solution(mesh):
    in_specs = (P("sample", "feat"), P("sample", "feat"))
    out_specs = (P(), P("sample", "feat"), P("sample", "feat"))
    return jax.shard_map(body, mesh=mesh, in_specs=in_specs, out_specs=out_specs, check_vma=False)
```

```python
import functools

import jax
import jax.numpy as jnp
from jax import lax
from jax.experimental import pallas as pl
from jax.experimental.pallas import tpu as pltpu
from jax.sharding import PartitionSpec as P

EPSILON = 1e-05
OFF_WEIGHT = 0.0051
BLOCK = 128
CORES = 2
MESH = pl.DeviceIdType.MESH


def kernel(
    groups,
    blocks,
    view_a,
    view_b,
    out_a,
    out_b,
    loss_out,
    raw,
    norm,
    scales,
    extra,
    acc,
    send_core,
    recv_core,
    send_first,
    recv_first,
    send_second,
    recv_second,
    gram,
    full,
    grads,
    products,
    loss_core,
    loss_sample,
    loss_depth,
    send_sem,
    recv_sem,
    local_sem,
):
    rows_dev, cols_dev = view_a.shape
    total_rows = rows_dev * groups
    width = cols_dev // groups
    depth = blocks // CORES
    inv_rows = 1.0 / total_rows
    n_blocks = total_rows // BLOCK
    used = n_blocks * (n_blocks + 1) // 2 * BLOCK
    packed = acc.shape[1]
    rows_core = packed // CORES
    rows_last = rows_core // (groups * depth)
    s = lax.axis_index("sample")
    f = lax.axis_index("feat")
    z = lax.div(f, CORES)
    c = lax.rem(f, CORES)
    other = 1 - c
    sample_peers = [(lax.rem(s + d, groups), f) for d in range(1, groups)]
    depth_peers = [(s, lax.rem(z + d, depth) * CORES + c) for d in range(1, depth)]
    sibling = (s, z * CORES + other)
    peers = sample_peers + depth_peers + [sibling]

    barrier = pltpu.get_barrier_semaphore()
    for peer in peers:
        pl.semaphore_signal(barrier, inc=1, device_id=peer, device_id_type=MESH)
    pl.semaphore_wait(barrier, len(peers))

    started = []

    def send(src, dst, peer):
        n = len(started)
        copy = pltpu.make_async_remote_copy(
            src_ref=src,
            dst_ref=dst,
            send_sem=send_sem.at[n],
            recv_sem=recv_sem.at[n],
            device_id=peer,
            device_id_type=MESH,
        )
        copy.start()
        started.append(copy)
        return copy

    def arrived(copies):
        for copy in copies:
            copy.wait_recv()

    def at(index, size):
        return pl.ds(pl.multiple_of(index * size, size), size)

    def send_view(v, view):
        copies = [
            send(view.at[:, at(peer[0], width)], raw.at[v, at(s, rows_dev), :], peer)
            for peer in sample_peers
        ]
        own = pltpu.make_async_copy(
            view.at[:, at(s, width)], raw.at[v, at(s, rows_dev), :], local_sem.at[v]
        )
        own.start()
        return copies, own

    weight = OFF_WEIGHT * inv_rows
    chunks = [slice(k, k + 64) for k in range(0, total_rows, 64)]

    def octets(x):
        return jnp.sum(x.reshape(x.shape[0] // 8, 8, x.shape[1]), axis=0)

    def normalize(v):
        total = jnp.zeros((8, width), jnp.float32)
        square = jnp.zeros((8, width), jnp.float32)
        for rows in chunks:
            x = raw[v, rows, :].astype(jnp.float32)
            total = total + octets(x)
            square = square + octets(x * x)
        mean = jnp.sum(total, axis=0, keepdims=True) * inv_rows
        square = jnp.sum(square, axis=0, keepdims=True) * inv_rows
        scale = lax.rsqrt(square - mean * mean + EPSILON)
        scales[v] = scale * weight
        for rows in chunks:
            x = raw[v, rows, :].astype(jnp.float32)
            norm[v, rows, :] = ((x - mean) * scale).astype(jnp.bfloat16)

    def spot(i, j):
        first = (i * (i + 1) // 2 + j) * BLOCK
        return slice(first, first + BLOCK)

    def reduce_core(v):
        if packed > used:
            send_core[v, used:, :] = jnp.zeros((packed - used, BLOCK), jnp.bfloat16)
            acc[v, used:, :] = jnp.zeros((packed - used, BLOCK), jnp.float32)
        for first in range(0, n_blocks, 2):
            last = min(first + 2, n_blocks)
            for left in range(0, last, 2):
                right = min(left + 2, last)
                square = lax.dot_general(
                    norm[v, first * BLOCK : last * BLOCK, :],
                    norm[v, left * BLOCK : right * BLOCK, :],
                    (((1,), (1,)), ((), ())),
                    preferred_element_type=jnp.float32,
                )
                for i in range(first, last):
                    for j in range(left, min(right, i + 1)):
                        tile = square[
                            (i - first) * BLOCK : (i - first + 1) * BLOCK,
                            (j - left) * BLOCK : (j - left + 1) * BLOCK,
                        ]
                        acc[v, spot(i, j), :] = tile
                        send_core[v, spot(i, j), :] = tile.astype(jnp.bfloat16)
        return [send(send_core.at[v, at(other, rows_core), :], recv_core.at[v], sibling)]

    def position(peer):
        return lax.div(peer[1], CORES)

    along = (
        (depth_peers, position, z, depth),
        (sample_peers, lambda peer: peer[0], s, groups),
    )

    def reduce_first(v):
        receivers, index, _, count = along[v]
        rows = rows_core // count
        mine = at(c, rows_core)
        total = acc[v, mine, :] + recv_core[v].astype(jnp.float32)
        acc[v, mine, :] = total
        send_first[v] = total.astype(jnp.bfloat16)
        return [
            send(send_first.at[v, at(index(peer), rows), :], recv_first.at[v, k, :rows], peer)
            for k, peer in enumerate(receivers)
        ]

    def reduce_second(v):
        _, _, me, count = along[v]
        receivers, index, _, _ = along[1 - v]
        rows = rows_core // count
        mine = at(c * count + me, rows)
        total = acc[v, mine, :]
        for k in range(count - 1):
            total = total + recv_first[v, k, :rows].astype(jnp.float32)
        acc[v, mine, :] = total
        send_second[v, :rows] = total.astype(jnp.bfloat16)
        return [
            send(send_second.at[v, at(index(peer), rows_last), :], recv_second.at[v, k], peer)
            for k, peer in enumerate(receivers)
        ]

    def spread(v, rows, receivers):
        here = gram.at[v, rows, :]
        return [send(here, here, peer) for peer in receivers]

    def gather_second(v):
        _, _, me, count = along[v]
        receivers, _, inner, inner_count = along[1 - v]
        mine = at((c * count + me) * inner_count + inner, rows_last)
        total = acc[v, mine, :]
        for k in range(inner_count - 1):
            total = total + recv_second[v, k].astype(jnp.float32)
        gram[v, mine, :] = total.astype(jnp.bfloat16)
        return spread(v, mine, receivers)

    def gather_first(v):
        receivers, _, me, count = along[v]
        return spread(v, at(c * count + me, rows_core // count), receivers)

    def gather_core(v):
        return spread(v, at(c, rows_core), [sibling])

    halves = [slice(k, min(k + 2 * BLOCK, width)) for k in range(0, width, 2 * BLOCK)]

    def return_grad(v, out):
        g = 1 - v
        for i in range(n_blocks):
            for j in range(i + 1):
                tile = gram[g, spot(i, j), :]
                full[i * BLOCK : (i + 1) * BLOCK, j * BLOCK : (j + 1) * BLOCK] = tile
                if j < i:
                    flipped = tile.astype(jnp.float32).T.astype(jnp.bfloat16)
                    full[j * BLOCK : (j + 1) * BLOCK, i * BLOCK : (i + 1) * BLOCK] = flipped
        copies = []
        for cs in halves:
            size = cs.stop - cs.start
            products[:, cs] = lax.dot_general(
                full[...],
                norm[v, :, cs],
                (((1,), (0,)), ((), ())),
                preferred_element_type=jnp.float32,
            )
            mean_grad = jnp.zeros((8, size), jnp.float32)
            mean_cross = jnp.zeros((8, size), jnp.float32)
            for rows in chunks:
                x = norm[v, rows, cs].astype(jnp.float32)
                y = norm[g, rows, cs].astype(jnp.float32)
                grad = products[rows, cs] + extra[:, cs] * y
                products[rows, cs] = grad
                mean_grad = mean_grad + octets(grad)
                mean_cross = mean_cross + octets(grad * x)
            mean_grad = jnp.sum(mean_grad, axis=0, keepdims=True) * inv_rows
            mean_cross = jnp.sum(mean_cross, axis=0, keepdims=True) * inv_rows
            scale = scales[v, :, cs]
            for rows in chunks:
                x = norm[v, rows, cs].astype(jnp.float32)
                grad = products[rows, cs] - mean_grad - x * mean_cross
                grads[v, rows, cs] = (scale * grad).astype(jnp.bfloat16)
            there = out.at[:, pl.ds(pl.multiple_of(s * width + cs.start, BLOCK), size)]
            copies += [
                send(grads.at[v, at(peer[0], rows_dev), cs], there, peer)
                for peer in sample_peers
            ]
        own = pltpu.make_async_copy(
            grads.at[v, at(s, rows_dev), :], out.at[:, at(s, width)], local_sem.at[2 + v]
        )
        own.start()
        return copies, own

    def fold(slots):
        total = slots[0]
        for k in range(1, slots.shape[0]):
            total = total + slots[k]
        return total

    copies_a, own_a = send_view(0, view_a)
    for copy in copies_a:
        copy.wait_send()
    copies_b, own_b = send_view(1, view_b)
    own_a.wait()
    arrived(copies_a)
    normalize(0)
    step_a = reduce_core(0)
    arrived(step_a)
    step_a = reduce_first(0)

    own_b.wait()
    arrived(copies_b)
    normalize(1)
    step_b = reduce_core(1)
    diag = jnp.zeros((8, width), jnp.float32)
    for rows in chunks:
        x = norm[0, rows, :].astype(jnp.float32) * norm[1, rows, :].astype(jnp.float32)
        diag = diag + octets(x)
    diag = jnp.sum(diag, axis=0, keepdims=True) * inv_rows
    extra[...] = ((1.0 - OFF_WEIGHT) * diag - 1.0) * (1.0 / weight)
    diag = (1.0 - diag) * (1.0 - diag) - OFF_WEIGHT * diag * diag
    part = jnp.zeros((1, BLOCK), jnp.float32)
    for k in range(0, width, BLOCK):
        part = part + diag[:, k : k + BLOCK]
    loss_core[c] = jnp.broadcast_to(part, (8, BLOCK))
    loss_copies = [send(loss_core.at[c], loss_core.at[c], sibling)]

    arrived(step_b)
    step_b = reduce_first(1)
    arrived(step_a)
    step_a = reduce_second(0)
    arrived(loss_copies)
    loss_sample[s] = fold(loss_core)
    loss_copies = [send(loss_sample.at[s], loss_sample.at[s], peer) for peer in sample_peers]
    arrived(step_a)
    step_a = gather_second(0)
    arrived(step_b)
    step_b = reduce_second(1)
    arrived(loss_copies)
    loss_depth[z] = fold(loss_sample)
    loss_copies = [send(loss_depth.at[z], loss_depth.at[z], peer) for peer in depth_peers]
    arrived(step_a)
    step_a = gather_first(0)
    arrived(step_b)
    step_b = gather_second(1)
    arrived(step_a)
    step_a = gather_core(0)
    arrived(step_b)
    step_b = gather_first(1)
    arrived(step_a)
    returning = [return_grad(1, out_b)]
    arrived(step_b)
    step_b = gather_core(1)
    arrived(step_b)
    returning.append(return_grad(0, out_a))

    arrived(loss_copies)
    product = jnp.zeros((BLOCK, BLOCK), jnp.float32)
    for i in range(n_blocks):
        for j in range(i + 1):
            pair = gram[0, spot(i, j), :].astype(jnp.float32) * gram[
                1, spot(i, j), :
            ].astype(jnp.float32)
            product = product + (pair if i == j else 2.0 * pair)
    trace = jnp.sum(product, axis=0, keepdims=True) * (OFF_WEIGHT * inv_rows * inv_rows)
    lane_loss = (fold(loss_depth)[0:1, :] + trace) * (1.0 / (cols_dev * blocks))
    loss_out[...] = jnp.sum(lane_loss, axis=1, keepdims=True)

    for copies, own in returning:
        own.wait()
        arrived(copies)
    for copy in started[len(copies_a) :]:
        copy.wait_send()


def body(view_a, view_b):
    rows_dev, cols_dev = view_a.shape
    groups = lax.axis_size("sample")
    blocks = lax.axis_size("feat")
    depth = blocks // CORES
    total_rows = rows_dev * groups
    width = cols_dev // groups
    n_blocks = total_rows // BLOCK
    step = CORES * groups * depth * 16
    packed = -(-(n_blocks * (n_blocks + 1) // 2 * BLOCK) // step) * step
    rows_core = packed // CORES
    rows_last = rows_core // (groups * depth)
    most, least = max(groups, depth), min(groups, depth)
    halves = -(-width // (2 * BLOCK))
    copies = (2 + 2 + 1 + 2 + 2 * halves) * (groups - 1) + 5 * (depth - 1) + 5
    bf16, f32 = jnp.bfloat16, jnp.float32
    vmem = pl.BlockSpec(memory_space=pltpu.VMEM)
    hbm = pl.BlockSpec(memory_space=pltpu.HBM)
    out_a, out_b, loss = pl.pallas_call(
        functools.partial(kernel, groups, blocks),
        out_shape=(
            jax.ShapeDtypeStruct((rows_dev, cols_dev), bf16),
            jax.ShapeDtypeStruct((rows_dev, cols_dev), bf16),
            jax.ShapeDtypeStruct((1, 1), f32),
        ),
        in_specs=[hbm, hbm],
        out_specs=(vmem, vmem, vmem),
        scratch_shapes=[
            pltpu.VMEM((2, total_rows, width), bf16),
            pltpu.VMEM((2, total_rows, width), bf16),
            pltpu.VMEM((2, 1, width), f32),
            pltpu.VMEM((1, width), f32),
            pltpu.VMEM((2, packed, BLOCK), f32),
            pltpu.VMEM((2, packed, BLOCK), bf16),
            pltpu.VMEM((2, rows_core, BLOCK), bf16),
            pltpu.VMEM((2, rows_core, BLOCK), bf16),
            pltpu.VMEM((2, most - 1, rows_core // least, BLOCK), bf16),
            pltpu.VMEM((2, rows_core // least, BLOCK), bf16),
            pltpu.VMEM((2, most - 1, rows_last, BLOCK), bf16),
            pltpu.VMEM((2, packed, BLOCK), bf16),
            pltpu.VMEM((total_rows, total_rows), bf16),
            pltpu.VMEM((2, total_rows, width), bf16),
            pltpu.VMEM((total_rows, width), f32),
            pltpu.VMEM((CORES, 8, BLOCK), f32),
            pltpu.VMEM((groups, 8, BLOCK), f32),
            pltpu.VMEM((depth, 8, BLOCK), f32),
            pltpu.SemaphoreType.DMA((copies,)),
            pltpu.SemaphoreType.DMA((copies,)),
            pltpu.SemaphoreType.DMA((4,)),
        ],
        compiler_params=pltpu.CompilerParams(
            collective_id=0, has_side_effects=True, vmem_limit_bytes=48 * 1024 * 1024
        ),
    )(
        pltpu.with_memory_space_constraint(view_a, pltpu.HBM),
        pltpu.with_memory_space_constraint(view_b, pltpu.HBM),
    )
    return (loss[0, 0], out_a, out_b)


def solution(mesh):
    in_specs = (P("sample", "feat"), P("sample", "feat"))
    out_specs = (P(), P("sample", "feat"), P("sample", "feat"))
    return jax.shard_map(body, mesh=mesh, in_specs=in_specs, out_specs=out_specs, check_vma=False)
```
